256 devices in a mesh: context: 64 (over z, x, core), channel: 4 (over y).
Axes of the slice: x: 4, y: 4, z: 8, core: 2. Of those that a mesh axis runs over, the one named last changes fastest.
Arguments:
- inputs: bfloat16 [2048, 16384], P('channel', 'context'), may hold values from -6 to 6
- out_grad: bfloat16 [2048, 16384], P('channel', 'context'), may hold values from -6 to 6
- low_pass: float32 [2, 2048], P(None, 'channel'), may hold values from 0.75 to 1.25
- high_pass: float32 [2, 2048], P(None, 'channel'), may hold values from -3 to 3
- level_weight: float32 [12, 2048], P(None, 'channel'), may hold values from -1.75 to 1.75
- mix: bfloat16 [2048, 2048], P(None, 'channel'), may hold values from -0.125 to 0.125
Outputs:
- grad_inputs: bfloat16 [2048, 16384], P('channel', 'context')
- grad_low: float32 [2, 2048], P(None, 'channel')
- grad_high: float32 [2, 2048], P(None, 'channel')
- grad_level: float32 [12, 2048], P(None, 'channel')
- grad_mix: float32 [2048, 2048], P('context', 'channel')
The draws below stay inside these ranges and needn't reach their ends.
All inputs are finite; a program needn't handle non-finite values.
Results may differ from the reference program's by a relative error of at most 0.012.
Values may be sent and summed in bfloat16 or wider, within the bound.
No kernel may reach another device: no remote copies, remote signals or barrier semaphores. Data moves between devices by JAX's collectives and lax.ppermute only.
A program may use at most 64 MiB of HBM per device.

```python
import jax
import jax.numpy as jnp
from jax import lax

D = 2048
LEVELS = 11
TOKENS = 16384
N_CHANNEL = 4


def steps_of(stream_key, shape, split, smallest, top_value):
    def one(position, blocks):
        heights = jax.random.uniform(jax.random.fold_in(jax.random.fold_in(stream_key, 6), position), (blocks,), jnp.float32, smallest / len(split), top_value / len(split))
        return jnp.repeat(jnp.exp(heights), shape[position] // blocks).reshape((-1,) + (1,) * (len(shape) - position - 1))

    factor_of = one(*split[0])
    for cut in split[1:]:
        factor_of = factor_of * one(*cut)
    return factor_of


def bell_draw(key, dims, scale, bound, pieces=(), kind=jnp.bfloat16):
    level = steps_of(key, dims, pieces, -0.22, 0.18) if pieces else 1.0
    drawn = jax.random.normal(key, dims, jnp.float32) * scale * level
    return jnp.minimum(jnp.maximum(drawn, -bound), bound).astype(kind)


def setup_inputs(seed: int = 0) -> dict:
    key_of = jax.random.split(jax.random.key(seed), 7)
    return {
        "inputs": bell_draw(key_of[0], (D, TOKENS), 1.0, 6.0, ((0, 4), (1, 64))),
        "out_grad": bell_draw(key_of[1], (D, TOKENS), 1.0, 6.0, ((0, 4), (1, 64))),
        "low_pass": jnp.clip(1.0 + 0.05 * jax.random.normal(key_of[2], (2, D), jnp.float32), 0.75, 1.25),
        "high_pass": bell_draw(key_of[3], (2, D), 1.0, 3.0, ((1, 4),), jnp.float32),
        "level_weight": bell_draw(key_of[4], (LEVELS + 1, D), (LEVELS + 1) ** -0.5, 1.75, ((1, 4),), jnp.float32),
        "mix": bell_draw(key_of[5], (D, D), D ** -0.5, 0.125, ((1, 4),)),
    }


HALF_ROOT = 0.5 ** 0.5

def later(values, distance):
    pad_zeros = jnp.zeros((values.shape[0], distance), values.dtype)
    return jnp.concatenate([pad_zeros, values[:, :values.shape[1] - distance]], 1)

def earlier(values, distance):
    pad_zeros = jnp.zeros((values.shape[0], distance), values.dtype)
    return jnp.concatenate([values[:, distance:], pad_zeros], 1)

def forward(present, low_taps, high_taps, weights):
    mixed_sum = jnp.zeros(present.shape, jnp.float32)
    pairs = []
    for level_index in range(LEVELS):
        lagged = later(present, 2 ** level_index)
        pairs.append((present, lagged))
        present_wide = present.astype(jnp.float32)
        lagged_wide = lagged.astype(jnp.float32)
        branch = HALF_ROOT * (high_taps[1 - 1] * present_wide + high_taps[1] * lagged_wide)
        present = (HALF_ROOT * (low_taps[0] * present_wide + low_taps[1] * lagged_wide)).astype(jnp.bfloat16)
        mixed_sum = mixed_sum + weights[level_index + 1] * branch
    mixed_sum = mixed_sum + weights[0] * present.astype(jnp.float32)
    return (mixed_sum, present, pairs)

def backward(args):
    present, grad_z, low_block, high_block, weight_block = args
    low_taps = low_block[:, :, None]
    high_taps = high_block[:, :, None]
    weights = weight_block[:, :, None]
    mixed_sum, last_level, pairs = forward(present, low_taps, high_taps, weights)
    grad_mixed = jax.vjp(jax.nn.gelu, mixed_sum)[1](grad_z)[0]
    low_acc = jnp.zeros((2, present.shape[0]), jnp.float32)
    high_acc = jnp.zeros((2, present.shape[0]), jnp.float32)
    rows_out = [None] * (LEVELS + 1)
    rows_out[0] = lax.optimization_barrier(jnp.sum(grad_mixed * last_level.astype(jnp.float32), 1))
    grad_now = weights[0] * grad_mixed
    for level_index in reversed(range(LEVELS)):
        level_now, lagged = pairs[level_index]
        present_wide = level_now.astype(jnp.float32)
        lagged_wide = lagged.astype(jnp.float32)
        grad_branch = weights[level_index + 1] * grad_mixed
        branch = HALF_ROOT * (high_taps[0] * present_wide + high_taps[1] * lagged_wide)
        low_acc = low_acc + HALF_ROOT * jnp.stack([lax.optimization_barrier(jnp.sum(present_wide * grad_now, 1)), lax.optimization_barrier(jnp.sum(lagged_wide * grad_now, 1))])
        high_acc = high_acc + HALF_ROOT * jnp.stack([lax.optimization_barrier(jnp.sum(present_wide * grad_branch, 1)), lax.optimization_barrier(jnp.sum(lagged_wide * grad_branch, 1))])
        rows_out[level_index + 1] = lax.optimization_barrier(jnp.sum(grad_mixed * branch, 1))
        direct_part = HALF_ROOT * (low_taps[0] * grad_now + high_taps[0] * grad_branch)
        lagged_part = HALF_ROOT * (low_taps[1] * grad_now + high_taps[1] * grad_branch)
        grad_now = direct_part + earlier(lagged_part, 2 ** level_index)
    return (grad_now.astype(jnp.bfloat16), low_acc, high_acc, jnp.stack(rows_out))

def reference(inputs, out_grad, low_pass, high_pass, level_weight, mix):
    block = D // (4 * N_CHANNEL)
    count = D // block

    def blocks_of(table):
        return table.reshape(table.shape[0], count, block).transpose(1, 0, 2)

    def unblock(table):
        return table.transpose(1, 0, 2).reshape(table.shape[1], D)
    inputs_blocks = inputs.reshape(count, block, TOKENS)
    low_blocks = blocks_of(low_pass)
    high_blocks = blocks_of(high_pass)
    weight_blocks = blocks_of(level_weight)

    def forward_z(args):
        present, low_block, high_block, weight_block = args
        mixed_sum = forward(present, low_block[:, :, None], high_block[:, :, None], weight_block[:, :, None])[0]
        return jax.nn.gelu(mixed_sum).astype(jnp.bfloat16)
    z_all = lax.map(forward_z, (inputs_blocks, low_blocks, high_blocks, weight_blocks)).reshape(D, TOKENS)
    scale = float(TOKENS) ** (-0.5)
    grad_mix = lax.dot_general(z_all, out_grad, (((1,), (1,)), ((), ())), preferred_element_type=jnp.float32) * scale
    grad_z = jnp.dot(mix, out_grad, preferred_element_type=jnp.float32)
    grad_x, low_grad, high_grad, level_grad = lax.map(backward, (inputs_blocks, grad_z.reshape(count, block, TOKENS), low_blocks, high_blocks, weight_blocks))
    return (grad_x.reshape(D, TOKENS), unblock(low_grad) * scale, unblock(high_grad) * scale, unblock(level_grad) * scale, grad_mix)
```

```python
import jax
import jax.numpy as jnp
from jax import lax
from jax.experimental import pallas as pl
from jax.experimental.pallas import tpu as pltpu
from jax.sharding import Mesh
from jax.sharding import PartitionSpec as P

R = 0.5**0.5
LEVELS = 11
CTX = ("z", "x", "core")
PLANE = ("x", "core")
NZ, NX, NC, NY = 8, 4, 2, 4
ROWS = 16
SPAN = 2048
STEP = 512
BLOCK = 256
ORDER = (0, 1, 3, 2)
F32, BF16 = jnp.float32, jnp.bfloat16
L0, L1, HP, HL, W0, H0, H1, WB = 0, 1, 2, 13, 24, 25, 26, 27
PARAMS = pltpu.CompilerParams(vmem_limit_bytes=12 * 1024 * 1024)


def shift(value, axis, steps, wrap=True):
    count = {"z": NZ, "x": NX, "core": NC, "y": NY}[axis]
    pairs = [(s, (s + steps) % count) for s in range(count) if wrap or 0 <= s + steps < count]
    return lax.ppermute(value, axis, pairs)


def forward_kernel(own_ref, halo_ref, coef_ref, z_ref, slope_ref, levels_ref, level, mixed):
    for block in range(8):
        columns = pl.ds(block * BLOCK, BLOCK)
        level[:, columns] = halo_ref[block].astype(F32)
        level[:, pl.ds(SPAN + block * BLOCK, BLOCK)] = own_ref[block].astype(F32)

    def column(index):
        return coef_ref[:, index : index + 1]

    for j in range(LEVELS):
        d = 2**j
        low0, low1 = column(L0), column(L1)
        high0, high1 = column(HP + j), column(HL + j)
        for chunk in reversed(range(2 * SPAN // STEP)):
            start = chunk * STEP
            if start + STEP <= 2 * d:
                continue
            present = level[:, pl.ds(start, STEP)]
            if d >= 128:
                if start >= d:
                    lagged = level[:, pl.ds(start - d, STEP)]
                else:
                    lagged = jnp.concatenate(
                        [level[:, pl.ds(start, d - start)], level[:, pl.ds(0, STEP - d + start)]], 1
                    ) if d - start < STEP else present
            elif start == 0:
                lagged = pltpu.roll(present, d, 1)
            else:
                lagged = pltpu.roll(level[:, pl.ds(start - 128, STEP + 128)], d, 1)[:, 128:]
            after = low0 * present + low1 * lagged
            if start >= SPAN:
                columns = pl.ds(start - SPAN, STEP)
                part = high0 * present + high1 * lagged
                if j > 0:
                    part = part + mixed[:, columns]
                if j == LEVELS - 1:
                    part = part + column(W0) * after
                    cube = part * part
                    inner = 0.7978845608028654 * part * (1.0 + 0.044715 * cube)
                    curve = jnp.tanh(inner)
                    cdf = 0.5 * (1.0 + curve)
                    slope = cdf + part * (0.5 * 0.7978845608028654) * (1.0 - curve * curve) * (
                        1.0 + 3 * 0.044715 * cube
                    )
                    z = (part * cdf).astype(BF16)
                    for piece in range(STEP // BLOCK):
                        block = (start - SPAN) // BLOCK + piece
                        inside = slice(piece * BLOCK, (piece + 1) * BLOCK)
                        z_ref[block] = z[:, inside]
                        slope_ref[block] = slope[:, inside]
                else:
                    mixed[:, columns] = part
                    stored = after.astype(BF16)
                    for piece in range(STEP // BLOCK):
                        block = (start - SPAN) // BLOCK + piece
                        inside = slice(piece * BLOCK, (piece + 1) * BLOCK)
                        levels_ref[j, block] = stored[:, inside]
            if j < LEVELS - 1:
                level[:, pl.ds(start, STEP)] = after


def forward(own, halo, coef):
    rows = pl.BlockSpec((8, ROWS, BLOCK), lambda g: (0, g, 0))
    return pl.pallas_call(
        forward_kernel,
        grid=(64 // ROWS,),
        in_specs=[rows, rows, pl.BlockSpec((ROWS, 128), lambda g: (g, 0))],
        out_specs=[rows, rows, pl.BlockSpec((LEVELS - 1, 8, ROWS, BLOCK), lambda g: (0, 0, g, 0))],
        out_shape=[
            jax.ShapeDtypeStruct((8, 64, BLOCK), BF16),
            jax.ShapeDtypeStruct((8, 64, BLOCK), F32),
            jax.ShapeDtypeStruct((LEVELS - 1, 8, 64, BLOCK), BF16),
        ],
        scratch_shapes=[pltpu.VMEM((ROWS, 2 * SPAN), F32), pltpu.VMEM((ROWS, SPAN), F32)],
        compiler_params=PARAMS,
        cost_estimate=pl.CostEstimate(flops=40_000_000, bytes_accessed=4_000_000, transcendentals=131072),
        name="forward_chain",
    )(own, halo, coef)


def backward_kernel(own_ref, halo_ref, inputs_ref, levels_ref, coef_ref, out_ref, grad, mixed, small):
    group = pl.program_id(0)
    channels = pl.ds(pl.multiple_of(group * ROWS, ROWS), ROWS)

    def column(index):
        return coef_ref[:, index : index + 1]

    weight0 = column(W0)
    for block in range(8):
        for ref, at in ((own_ref, 0), (halo_ref, SPAN)):
            columns = pl.ds(at + block * BLOCK, BLOCK)
            value = ref[block].astype(F32)
            mixed[:, columns] = value
            grad[:, columns] = weight0 * value

    lanes = (ROWS, 128)

    def folded(value):
        total = value[:, :128]
        for at in range(128, value.shape[1], 128):
            total = total + value[:, at : at + 128]
        return total

    low_sums = [jnp.zeros(lanes, F32), jnp.zeros(lanes, F32)]
    high_sums = [jnp.zeros(lanes, F32), jnp.zeros(lanes, F32)]
    level_sums = [None] * (LEVELS + 1)
    for j in reversed(range(LEVELS)):
        d = 2**j
        low0, low1 = column(L0), column(L1)
        high0, high1 = column(HP + j), column(HL + j)
        weight = column(WB + j)
        gm_now = jnp.zeros(lanes, F32)
        gm_lag = jnp.zeros(lanes, F32)
        need = SPAN + (d if j else 0)
        need = -(-need // 128) * 128
        for start in range(0, need, STEP):
            size = min(STEP, need - start)
            window = pl.ds(start, size)
            g, m = grad[:, window], mixed[:, window]
            if d >= 128:
                g_next, m_next = grad[:, pl.ds(start + d, size)], mixed[:, pl.ds(start + d, size)]
            else:
                wide = pl.ds(start, size + 128)
                g_next = pltpu.roll(grad[:, wide], size + 128 - d, 1)[:, :size]
                m_next = pltpu.roll(mixed[:, wide], size + 128 - d, 1)[:, :size]
            if start < SPAN:
                pieces = []
                for piece in range(STEP // BLOCK):
                    block = start // BLOCK + piece
                    pieces.append(inputs_ref[block] if j == 0 else levels_ref[j - 1, block])
                value = jnp.concatenate(pieces, 1).astype(F32)
                low_sums[0] = low_sums[0] + folded(value * g)
                low_sums[1] = low_sums[1] + folded(value * g_next)
                gm_now = gm_now + folded(value * m)
                gm_lag = gm_lag + folded(value * m_next)
            after = low0 * g + high0 * m + low1 * g_next + high1 * m_next
            if j == 0:
                after = after.astype(BF16)
                for piece in range(STEP // BLOCK):
                    block = start // BLOCK + piece
                    out_ref[block, channels] = after[:, piece * BLOCK : (piece + 1) * BLOCK]
            else:
                grad[:, window] = after
        high_sums[0] = high_sums[0] + weight * gm_now
        high_sums[1] = high_sums[1] + weight * gm_lag
        level_sums[j + 1] = column(H0) * gm_now + column(H1) * gm_lag
        if j == LEVELS - 1:
            level_sums[0] = low0 * gm_now + low1 * gm_lag
    scale = float(NZ * SPAN) ** (-0.5)
    every = [s * (R * scale) for s in low_sums + high_sums] + [s * scale for s in level_sums]
    lane = lax.broadcasted_iota(jnp.int32, (ROWS, BLOCK), 1) - group * len(every)
    found = jnp.zeros((ROWS, BLOCK), F32)
    for k, value in enumerate(every):
        found = jnp.where(lane == k, jnp.sum(value, 1, keepdims=True), found)

    @pl.when(group == 0)
    def _():
        small[...] = found

    @pl.when(group > 0)
    def _():
        small[...] = small[...] + found

    @pl.when(group == 64 // ROWS - 1)
    def _():
        for block in range(8):
            out_ref[block, 64:] = small[...].astype(BF16)


def backward(own, halo, inputs, levels, coef):
    rows = pl.BlockSpec((8, ROWS, BLOCK), lambda g: (0, g, 0))
    return pl.pallas_call(
        backward_kernel,
        grid=(64 // ROWS,),
        in_specs=[
            rows,
            rows,
            rows,
            pl.BlockSpec((LEVELS - 1, 8, ROWS, BLOCK), lambda g: (0, 0, g, 0)),
            pl.BlockSpec((ROWS, 128), lambda g: (g, 0)),
        ],
        out_specs=pl.BlockSpec((8, 64 + ROWS, BLOCK), lambda g: (0, 0, 0)),
        out_shape=jax.ShapeDtypeStruct((8, 64 + ROWS, BLOCK), BF16),
        scratch_shapes=[
            pltpu.VMEM((ROWS, 2 * SPAN), F32),
            pltpu.VMEM((ROWS, 2 * SPAN), F32),
            pltpu.VMEM((ROWS, BLOCK), F32),
        ],
        compiler_params=PARAMS,
        cost_estimate=pl.CostEstimate(flops=40_000_000, bytes_accessed=4_000_000, transcendentals=0),
        name="backward_chain",
    )(own, halo, inputs, levels, coef)


def product_kernel(place_ref, *refs):
    z_refs, og_refs, out_ref, rows, total = refs[:4], refs[4:12], refs[12], refs[13], refs[14]
    y, x, core = place_ref[0], place_ref[1], place_ref[2]
    for k, steps in enumerate(ORDER):
        source = lax.rem(y + (NY - steps), NY)
        for block in range(8):
            rows[block, pl.ds(pl.multiple_of(source * 64, 64), 64), :] = z_refs[k][block]
    for k in range(8):
        steps, flip = ORDER[k // 2], k % 2
        block = lax.rem(x + (NX - steps), NX) * 2 + (core if flip == 0 else 1 - core)
        part = lax.dot_general(
            rows[block], og_refs[k][...], (((1,), (1,)), ((), ())), preferred_element_type=F32
        )
        total[...] = part if k == 0 else total[...] + part
    scale = float(NZ * SPAN) ** (-0.5)
    for chunk in range(8):
        out_ref[chunk, :32] = (total[chunk * 32 : (chunk + 1) * 32] * scale).astype(BF16)


def product(place, z_pieces, og_pieces):
    whole = pl.BlockSpec(memory_space=pltpu.VMEM)
    return pl.pallas_call(
        product_kernel,
        in_specs=[pl.BlockSpec(memory_space=pltpu.SMEM)] + [whole] * 12,
        out_specs=whole,
        out_shape=jax.ShapeDtypeStruct((8, 32 + ROWS, 512), BF16),
        scratch_shapes=[pltpu.VMEM((8, 256, BLOCK), BF16), pltpu.VMEM((256, 512), F32)],
        compiler_params=PARAMS,
        cost_estimate=pl.CostEstimate(flops=540_000_000, bytes_accessed=4_000_000, transcendentals=0),
        name="mix_product",
    )(place, *z_pieces, *og_pieces)


def partials_kernel(place_ref, mix_ref, og_ref, one_ref, three_ref, two_ref, own_ref):
    y = place_ref[0]
    for steps, ref in ((1, one_ref), (3, three_ref), (2, two_ref), (0, own_ref)):
        start = pl.multiple_of(lax.rem(y + steps, NY) * 512, 512)
        part = jnp.dot(mix_ref[pl.ds(start, 512), :], og_ref[...], preferred_element_type=F32)
        ref[...] = part.astype(ref.dtype)


def partials(place, mix, out_grad):
    whole = pl.BlockSpec(memory_space=pltpu.VMEM)
    return pl.pallas_call(
        partials_kernel,
        in_specs=[pl.BlockSpec(memory_space=pltpu.SMEM), whole, whole],
        out_specs=[whole] * 4,
        out_shape=[jax.ShapeDtypeStruct((512, BLOCK), BF16)] * 3 + [jax.ShapeDtypeStruct((512, BLOCK), F32)],
        compiler_params=PARAMS,
        cost_estimate=pl.CostEstimate(flops=1_080_000_000, bytes_accessed=3_500_000, transcendentals=0),
        name="grad_z_partials",
    )(place, mix, out_grad)


def spread_kernel(*refs):
    ins, out_ref = refs[:-1], refs[-1]
    for half in range(2):
        for block in range(8):
            rows = pl.ds(half * 256 + block * 32, 32)
            total = ins[0][rows, :]
            for ref in ins[1:]:
                total = total + ref[rows, :].astype(F32)
            out_ref[block, half * 32 : (half + 1) * 32] = total.astype(BF16)


def spread(*values):
    whole = pl.BlockSpec(memory_space=pltpu.VMEM)
    return pl.pallas_call(
        spread_kernel,
        in_specs=[whole] * len(values),
        out_specs=whole,
        out_shape=jax.ShapeDtypeStruct((8, 64, BLOCK), BF16),
        compiler_params=PARAMS,
        cost_estimate=pl.CostEstimate(flops=500_000, bytes_accessed=1_000_000, transcendentals=0),
        name="rows_by_device",
    )(*values)


def gather_kernel(in_ref, out_ref):
    for half in range(2):
        for block in range(8):
            rows = pl.ds(half * 256 + block * 32, 32)
            out_ref[rows, :] = in_ref[block, half * 32 : (half + 1) * 32]


def gathered(value):
    whole = pl.BlockSpec(memory_space=pltpu.VMEM)
    return pl.pallas_call(
        gather_kernel,
        in_specs=[whole],
        out_specs=whole,
        out_shape=jax.ShapeDtypeStruct((512, BLOCK), BF16),
        compiler_params=PARAMS,
        cost_estimate=pl.CostEstimate(flops=0, bytes_accessed=600_000, transcendentals=0),
        name="grad_inputs_rows",
    )(value)


def pack_kernel(part_ref, sums_ref, out_ref):
    pieces = []
    for pair in range(4):
        odd = pltpu.roll(sums_ref[2 * pair + 1].astype(F32), 64, 1)
        pieces.append((sums_ref[2 * pair].astype(F32) + odd).astype(BF16))
    packed = jnp.concatenate(pieces, 1)
    for plane in range(NZ):
        out_ref[plane] = packed


def packed(part, grad_in):
    return pl.pallas_call(
        pack_kernel,
        grid=(1,),
        in_specs=[
            pl.BlockSpec(memory_space=pl.ANY),
            pl.BlockSpec((8, ROWS, 128), lambda g: (0, 64 // ROWS, 0)),
        ],
        out_specs=pl.BlockSpec((NZ, ROWS, 512), lambda g: (0, 32 // ROWS, 0)),
        out_shape=jax.ShapeDtypeStruct((NZ, 32 + ROWS, 512), BF16),
        input_output_aliases={0: 0},
        compiler_params=PARAMS,
        cost_estimate=pl.CostEstimate(flops=20_000, bytes_accessed=200_000, transcendentals=0),
        name="pack_sums",
    )(part, grad_in)


def sums_kernel(in_ref, mix_ref, low_ref, high_ref, level_ref):
    total = in_ref[0].astype(F32)
    for plane in range(1, NZ):
        total = total + in_ref[plane].astype(F32)
    mix_ref[...] = total[:32]
    for pair in range(4):
        turned = total[32:, pair * 128 : (pair + 1) * 128].T
        for odd in range(2):
            for group in range(64 // ROWS):
                at = (group // 2) * 256 + (2 * pair + odd) * 32 + (group % 2) * ROWS
                part = turned[odd * 64 + group * 16 : odd * 64 + (group + 1) * 16]
                low_ref[:, at : at + ROWS] = part[:2]
                high_ref[:, at : at + ROWS] = part[2:4]
                level_ref[:, at : at + ROWS] = part[4:]


def plane_sums(value):
    whole = pl.BlockSpec(memory_space=pltpu.VMEM)
    return pl.pallas_call(
        sums_kernel,
        in_specs=[whole],
        out_specs=[whole] * 4,
        out_shape=[jax.ShapeDtypeStruct((rows, 512), F32) for rows in (32, 2, 2, 12)],
        compiler_params=PARAMS,
        cost_estimate=pl.CostEstimate(flops=200_000, bytes_accessed=450_000, transcendentals=0),
        name="plane_sums",
    )(value)


def exchanged(value, axes):
    return lax.all_to_all(value, axes, 0, 0, tiled=True)


def after(value, *others):
    return lax.optimization_barrier((value, *others))[0]


def shards(inputs, out_grad, low_pass, high_pass, level_weight, mix):
    y, x, core = lax.axis_index("y"), lax.axis_index("x"), lax.axis_index("core")
    mine = x * NC + core
    place = jnp.stack([y, x, core]).astype(jnp.int32)

    one, three, two, grad_z = partials(place, mix, out_grad)
    arrived = [shift(value, "y", steps) for value, steps in ((one, 1), (three, 3), (two, 2))]

    own = exchanged(spread(after(inputs, grad_z)), PLANE)
    halo = shift(own, "z", 1, wrap=False)
    grad_z = exchanged(spread(grad_z, *arrived), PLANE)

    og_x = [out_grad] + [shift(out_grad, "x", steps) for steps in (1, 3)]
    og_x += [shift(after(out_grad, own), "x", 2)]

    own_rows = [low_pass * R, level_weight[1:] * (R * high_pass[0]), level_weight[1:] * (R * high_pass[1])]
    own_rows += [level_weight[:1], R * high_pass, level_weight[1:]]
    table = jnp.concatenate(own_rows, 0)
    table = lax.dynamic_slice_in_dim(table.reshape(-1, 2, 8, 32), mine, 1, 2).reshape(-1, 64)
    coef = jnp.pad(table, ((0, 128 - table.shape[0]), (0, 0))).T

    z, slope, levels = forward(own, halo, coef)
    z_all = [z] + [shift(z, "y", steps) for steps in (1, 3, 2)]

    grad_mixed = (grad_z.astype(F32) * slope).astype(BF16)
    grad_halo = shift(grad_mixed, "z", -1, wrap=False)
    grad_in = backward(grad_mixed, grad_halo, own, levels, coef)
    og = []
    for piece in og_x:
        og += [piece, shift(after(piece, grad_in), "core", 1)]
    grad_in = exchanged(grad_in, PLANE)
    part = product(place, z_all, og)
    grad_mix, low, high, level = plane_sums(exchanged(packed(part, grad_in), "z"))
    return gathered(grad_in), low, high, level, grad_mix


def solution(mesh):
    mesh = Mesh(mesh.devices.reshape(NZ, NX, NC, NY), ("z", "x", "core", "y"))
    wide, tall = P("y", CTX), P(None, "y")
    return jax.shard_map(
        shards,
        mesh=mesh,
        in_specs=(wide, wide, tall, tall, tall, tall),
        out_specs=(wide, tall, tall, tall, P(CTX, "y")),
        check_vma=False,
    )
```

```python
import jax
import jax.numpy as jnp
from jax import lax
from jax.experimental import pallas as pl
from jax.experimental.pallas import tpu as pltpu
from jax.sharding import Mesh
from jax.sharding import PartitionSpec as P

R = 0.5**0.5
LEVELS = 11
CTX = ("z", "x", "core")
PLANE = ("x", "core")
NZ, NX, NC, NY = 8, 4, 2, 4
ROWS = 16
SPAN = 2048
STEP = 512
BLOCK = 256
ORDER = (0, 1, 3, 2)
F32, BF16 = jnp.float32, jnp.bfloat16
L0, L1, HP, HL, W0, H0, H1, WB = 0, 1, 2, 13, 24, 25, 26, 27
PARAMS = pltpu.CompilerParams(vmem_limit_bytes=12 * 1024 * 1024)


def shift(value, axis, steps, wrap=True):
    count = {"z": NZ, "x": NX, "core": NC, "y": NY}[axis]
    pairs = [(s, (s + steps) % count) for s in range(count) if wrap or 0 <= s + steps < count]
    return lax.ppermute(value, axis, pairs)


def forward_kernel(own_ref, halo_any, coef_ref, z_ref, slope_ref, levels_ref, level, mixed, halo_ref, sems):
    group = pl.program_id(0)

    def arriving(at):
        rows = pl.ds(pl.multiple_of(at * ROWS, ROWS), ROWS)
        return pltpu.make_async_copy(halo_any.at[:, rows, :], halo_ref.at[at], sems.at[at])

    @pl.when(group == 0)
    def _():
        for at in range(64 // ROWS):
            arriving(at).start()

    for block in range(8):
        level[:, pl.ds(SPAN + block * BLOCK, BLOCK)] = own_ref[block].astype(F32)
    arriving(group).wait()
    for block in range(8):
        level[:, pl.ds(block * BLOCK, BLOCK)] = halo_ref[group, block].astype(F32)

    def column(index):
        return coef_ref[:, index : index + 1]

    for j in range(LEVELS):
        d = 2**j
        low0, low1 = column(L0), column(L1)
        high0, high1 = column(HP + j), column(HL + j)
        for chunk in reversed(range(2 * SPAN // STEP)):
            start = chunk * STEP
            if start + STEP <= 2 * d:
                continue
            present = level[:, pl.ds(start, STEP)]
            if d >= 128:
                if start >= d:
                    lagged = level[:, pl.ds(start - d, STEP)]
                else:
                    lagged = jnp.concatenate(
                        [level[:, pl.ds(start, d - start)], level[:, pl.ds(0, STEP - d + start)]], 1
                    ) if d - start < STEP else present
            elif start == 0:
                lagged = pltpu.roll(present, d, 1)
            else:
                lagged = pltpu.roll(level[:, pl.ds(start - 128, STEP + 128)], d, 1)[:, 128:]
            after = low0 * present + low1 * lagged
            if start >= SPAN:
                columns = pl.ds(start - SPAN, STEP)
                part = high0 * present + high1 * lagged
                if j > 0:
                    part = part + mixed[:, columns]
                if j == LEVELS - 1:
                    part = part + column(W0) * after
                    cube = part * part
                    inner = 0.7978845608028654 * part * (1.0 + 0.044715 * cube)
                    curve = jnp.tanh(inner)
                    cdf = 0.5 * (1.0 + curve)
                    slope = cdf + part * (0.5 * 0.7978845608028654) * (1.0 - curve * curve) * (
                        1.0 + 3 * 0.044715 * cube
                    )
                    z = (part * cdf).astype(BF16)
                    for piece in range(STEP // BLOCK):
                        block = (start - SPAN) // BLOCK + piece
                        inside = slice(piece * BLOCK, (piece + 1) * BLOCK)
                        z_ref[block] = z[:, inside]
                        slope_ref[block] = slope[:, inside]
                else:
                    mixed[:, columns] = part
                    stored = after.astype(BF16)
                    for piece in range(STEP // BLOCK):
                        block = (start - SPAN) // BLOCK + piece
                        inside = slice(piece * BLOCK, (piece + 1) * BLOCK)
                        levels_ref[j, block] = stored[:, inside]
            if j < LEVELS - 1:
                level[:, pl.ds(start, STEP)] = after


def in_hbm(value):
    return pltpu.with_memory_space_constraint(value, pltpu.HBM)


def forward(own, halo, coef):
    rows = pl.BlockSpec((8, ROWS, BLOCK), lambda g: (0, g, 0))
    return pl.pallas_call(
        forward_kernel,
        grid=(64 // ROWS,),
        in_specs=[rows, pl.BlockSpec(memory_space=pl.ANY), pl.BlockSpec((ROWS, 128), lambda g: (g, 0))],
        out_specs=[rows, rows, pl.BlockSpec((LEVELS - 1, 8, ROWS, BLOCK), lambda g: (0, 0, g, 0))],
        out_shape=[
            pltpu.HBM((8, 64, BLOCK), BF16),
            jax.ShapeDtypeStruct((8, 64, BLOCK), F32),
            jax.ShapeDtypeStruct((LEVELS - 1, 8, 64, BLOCK), BF16),
        ],
        scratch_shapes=[
            pltpu.VMEM((ROWS, 2 * SPAN), F32),
            pltpu.VMEM((ROWS, SPAN), F32),
            pltpu.VMEM((64 // ROWS, 8, ROWS, BLOCK), BF16),
            pltpu.SemaphoreType.DMA((64 // ROWS,)),
        ],
        compiler_params=PARAMS,
        cost_estimate=pl.CostEstimate(flops=40_000_000, bytes_accessed=4_000_000, transcendentals=131072),
        name="forward_chain",
    )(own, in_hbm(halo), coef)


def backward_kernel(own_ref, halo_ref, inputs_ref, levels_ref, coef_ref, out_ref, grad, mixed, small):
    group = pl.program_id(0)
    channels = pl.ds(pl.multiple_of(group * ROWS, ROWS), ROWS)

    def column(index):
        return coef_ref[:, index : index + 1]

    weight0 = column(W0)
    for block in range(8):
        for ref, at in ((own_ref, 0), (halo_ref, SPAN)):
            columns = pl.ds(at + block * BLOCK, BLOCK)
            value = ref[block].astype(F32)
            mixed[:, columns] = value
            grad[:, columns] = weight0 * value

    lanes = (ROWS, 128)

    def folded(value):
        total = value[:, :128]
        for at in range(128, value.shape[1], 128):
            total = total + value[:, at : at + 128]
        return total

    low_sums = [jnp.zeros(lanes, F32), jnp.zeros(lanes, F32)]
    high_sums = [jnp.zeros(lanes, F32), jnp.zeros(lanes, F32)]
    level_sums = [None] * (LEVELS + 1)
    for j in reversed(range(LEVELS)):
        d = 2**j
        low0, low1 = column(L0), column(L1)
        high0, high1 = column(HP + j), column(HL + j)
        weight = column(WB + j)
        gm_now = jnp.zeros(lanes, F32)
        gm_lag = jnp.zeros(lanes, F32)
        need = SPAN + (d if j else 0)
        need = -(-need // 128) * 128
        for start in range(0, need, STEP):
            size = min(STEP, need - start)
            window = pl.ds(start, size)
            g, m = grad[:, window], mixed[:, window]
            if d >= 128:
                g_next, m_next = grad[:, pl.ds(start + d, size)], mixed[:, pl.ds(start + d, size)]
            else:
                wide = pl.ds(start, size + 128)
                g_next = pltpu.roll(grad[:, wide], size + 128 - d, 1)[:, :size]
                m_next = pltpu.roll(mixed[:, wide], size + 128 - d, 1)[:, :size]
            if start < SPAN:
                pieces = []
                for piece in range(STEP // BLOCK):
                    block = start // BLOCK + piece
                    pieces.append(inputs_ref[block] if j == 0 else levels_ref[j - 1, block])
                value = jnp.concatenate(pieces, 1).astype(F32)
                low_sums[0] = low_sums[0] + folded(value * g)
                low_sums[1] = low_sums[1] + folded(value * g_next)
                gm_now = gm_now + folded(value * m)
                gm_lag = gm_lag + folded(value * m_next)
            after = low0 * g + high0 * m + low1 * g_next + high1 * m_next
            if j == 0:
                after = after.astype(BF16)
                for piece in range(STEP // BLOCK):
                    block = start // BLOCK + piece
                    out_ref[block, channels] = after[:, piece * BLOCK : (piece + 1) * BLOCK]
            else:
                grad[:, window] = after
        high_sums[0] = high_sums[0] + weight * gm_now
        high_sums[1] = high_sums[1] + weight * gm_lag
        level_sums[j + 1] = column(H0) * gm_now + column(H1) * gm_lag
        if j == LEVELS - 1:
            level_sums[0] = low0 * gm_now + low1 * gm_lag
    scale = float(NZ * SPAN) ** (-0.5)
    every = [s * (R * scale) for s in low_sums + high_sums] + [s * scale for s in level_sums]
    lane = lax.broadcasted_iota(jnp.int32, (ROWS, BLOCK), 1) - group * len(every)
    found = jnp.zeros((ROWS, BLOCK), F32)
    for k, value in enumerate(every):
        found = jnp.where(lane == k, jnp.sum(value, 1, keepdims=True), found)

    @pl.when(group == 0)
    def _():
        small[...] = found

    @pl.when(group > 0)
    def _():
        small[...] = small[...] + found

    @pl.when(group == 64 // ROWS - 1)
    def _():
        for block in range(8):
            out_ref[block, 64:] = small[...].astype(BF16)


def backward(own, halo, inputs, levels, coef):
    rows = pl.BlockSpec((8, ROWS, BLOCK), lambda g: (0, g, 0))
    return pl.pallas_call(
        backward_kernel,
        grid=(64 // ROWS,),
        in_specs=[
            rows,
            rows,
            rows,
            pl.BlockSpec((LEVELS - 1, 8, ROWS, BLOCK), lambda g: (0, 0, g, 0)),
            pl.BlockSpec((ROWS, 128), lambda g: (g, 0)),
        ],
        out_specs=pl.BlockSpec((8, 64 + ROWS, BLOCK), lambda g: (0, 0, 0)),
        out_shape=jax.ShapeDtypeStruct((8, 64 + ROWS, BLOCK), BF16),
        scratch_shapes=[
            pltpu.VMEM((ROWS, 2 * SPAN), F32),
            pltpu.VMEM((ROWS, 2 * SPAN), F32),
            pltpu.VMEM((ROWS, BLOCK), F32),
        ],
        compiler_params=PARAMS,
        cost_estimate=pl.CostEstimate(flops=40_000_000, bytes_accessed=4_000_000, transcendentals=0),
        name="backward_chain",
    )(own, halo, inputs, levels, coef)


def product_kernel(place_ref, *refs):
    z_refs, og_refs, out_ref = refs[:4], refs[4:12], refs[12]
    rows, out_grads, total, z_sem, og_sem = refs[13:]
    y, x, core = place_ref[0], place_ref[1], place_ref[2]
    copies = []
    for k, steps in enumerate(ORDER):
        source = pl.multiple_of(lax.rem(y + (NY - steps), NY) * 64, 64)
        copies.append(pltpu.make_async_copy(z_refs[k], rows.at[:, pl.ds(source, 64), :], z_sem.at[k]))
    for k in range(8):
        steps, flip = ORDER[k // 2], k % 2
        block = lax.rem(x + (NX - steps), NX) * 2 + (core if flip == 0 else 1 - core)
        copies.append(pltpu.make_async_copy(og_refs[k], out_grads.at[block], og_sem.at[k]))
    for copy in copies:
        copy.start()
    for copy in copies:
        copy.wait()
    for block in range(8):
        part = lax.dot_general(
            rows[block], out_grads[block], (((1,), (1,)), ((), ())), preferred_element_type=F32
        )
        total[...] = part if block == 0 else total[...] + part
    scale = float(NZ * SPAN) ** (-0.5)
    for chunk in range(8):
        out_ref[chunk, :32] = (total[chunk * 32 : (chunk + 1) * 32] * scale).astype(BF16)


def product(place, z_pieces, og_pieces):
    anywhere = pl.BlockSpec(memory_space=pl.ANY)
    return pl.pallas_call(
        product_kernel,
        in_specs=[pl.BlockSpec(memory_space=pltpu.SMEM)] + [anywhere] * 12,
        out_specs=pl.BlockSpec(memory_space=pltpu.VMEM),
        out_shape=jax.ShapeDtypeStruct((8, 32 + ROWS, 512), BF16),
        scratch_shapes=[
            pltpu.VMEM((8, 256, BLOCK), BF16),
            pltpu.VMEM((8, 512, BLOCK), BF16),
            pltpu.VMEM((256, 512), F32),
            pltpu.SemaphoreType.DMA((4,)),
            pltpu.SemaphoreType.DMA((8,)),
        ],
        compiler_params=PARAMS,
        cost_estimate=pl.CostEstimate(flops=540_000_000, bytes_accessed=4_000_000, transcendentals=0),
        name="mix_product",
    )(place, *map(in_hbm, z_pieces), *map(in_hbm, og_pieces))


def partials_kernel(place_ref, mix_ref, og_ref, one_ref, three_ref, two_ref, own_ref):
    y = place_ref[0]
    for steps, ref in ((1, one_ref), (3, three_ref), (2, two_ref), (0, own_ref)):
        start = pl.multiple_of(lax.rem(y + steps, NY) * 512, 512)
        part = jnp.dot(mix_ref[pl.ds(start, 512), :], og_ref[...], preferred_element_type=F32)
        ref[...] = part.astype(ref.dtype)


def partials(place, mix, out_grad):
    whole = pl.BlockSpec(memory_space=pltpu.VMEM)
    return pl.pallas_call(
        partials_kernel,
        in_specs=[pl.BlockSpec(memory_space=pltpu.SMEM), whole, whole],
        out_specs=[whole] * 4,
        out_shape=[jax.ShapeDtypeStruct((512, BLOCK), BF16)] * 3 + [jax.ShapeDtypeStruct((512, BLOCK), F32)],
        compiler_params=PARAMS,
        cost_estimate=pl.CostEstimate(flops=1_080_000_000, bytes_accessed=3_500_000, transcendentals=0),
        name="grad_z_partials",
    )(place, mix, out_grad)


def spread_kernel(*refs):
    ins, out_ref = refs[:-1], refs[-1]
    for half in range(2):
        for block in range(8):
            rows = pl.ds(half * 256 + block * 32, 32)
            total = ins[0][rows, :]
            for ref in ins[1:]:
                total = total + ref[rows, :].astype(F32)
            out_ref[block, half * 32 : (half + 1) * 32] = total.astype(BF16)


def spread(*values):
    whole = pl.BlockSpec(memory_space=pltpu.VMEM)
    return pl.pallas_call(
        spread_kernel,
        in_specs=[whole] * len(values),
        out_specs=whole,
        out_shape=jax.ShapeDtypeStruct((8, 64, BLOCK), BF16),
        compiler_params=PARAMS,
        cost_estimate=pl.CostEstimate(flops=500_000, bytes_accessed=1_000_000, transcendentals=0),
        name="rows_by_device",
    )(*values)


def gather_kernel(in_ref, out_ref):
    for half in range(2):
        for block in range(8):
            rows = pl.ds(half * 256 + block * 32, 32)
            out_ref[rows, :] = in_ref[block, half * 32 : (half + 1) * 32]


def gathered(value):
    whole = pl.BlockSpec(memory_space=pltpu.VMEM)
    return pl.pallas_call(
        gather_kernel,
        in_specs=[whole],
        out_specs=whole,
        out_shape=jax.ShapeDtypeStruct((512, BLOCK), BF16),
        compiler_params=PARAMS,
        cost_estimate=pl.CostEstimate(flops=0, bytes_accessed=600_000, transcendentals=0),
        name="grad_inputs_rows",
    )(value)


def pack_kernel(part_ref, sums_ref, out_ref):
    pieces = []
    for pair in range(4):
        odd = pltpu.roll(sums_ref[2 * pair + 1].astype(F32), 64, 1)
        pieces.append((sums_ref[2 * pair].astype(F32) + odd).astype(BF16))
    packed = jnp.concatenate(pieces, 1)
    for plane in range(NZ):
        out_ref[plane] = packed


def packed(part, grad_in):
    return pl.pallas_call(
        pack_kernel,
        grid=(1,),
        in_specs=[
            pl.BlockSpec(memory_space=pl.ANY),
            pl.BlockSpec((8, ROWS, 128), lambda g: (0, 64 // ROWS, 0)),
        ],
        out_specs=pl.BlockSpec((NZ, ROWS, 512), lambda g: (0, 32 // ROWS, 0)),
        out_shape=jax.ShapeDtypeStruct((NZ, 32 + ROWS, 512), BF16),
        input_output_aliases={0: 0},
        compiler_params=PARAMS,
        cost_estimate=pl.CostEstimate(flops=20_000, bytes_accessed=200_000, transcendentals=0),
        name="pack_sums",
    )(part, grad_in)


def sums_kernel(in_ref, mix_ref, low_ref, high_ref, level_ref):
    total = in_ref[0].astype(F32)
    for plane in range(1, NZ):
        total = total + in_ref[plane].astype(F32)
    mix_ref[...] = total[:32]
    for pair in range(4):
        turned = total[32:, pair * 128 : (pair + 1) * 128].T
        for odd in range(2):
            for group in range(64 // ROWS):
                at = (group // 2) * 256 + (2 * pair + odd) * 32 + (group % 2) * ROWS
                part = turned[odd * 64 + group * 16 : odd * 64 + (group + 1) * 16]
                low_ref[:, at : at + ROWS] = part[:2]
                high_ref[:, at : at + ROWS] = part[2:4]
                level_ref[:, at : at + ROWS] = part[4:]


def plane_sums(value):
    whole = pl.BlockSpec(memory_space=pltpu.VMEM)
    return pl.pallas_call(
        sums_kernel,
        in_specs=[whole],
        out_specs=[whole] * 4,
        out_shape=[jax.ShapeDtypeStruct((rows, 512), F32) for rows in (32, 2, 2, 12)],
        compiler_params=PARAMS,
        cost_estimate=pl.CostEstimate(flops=200_000, bytes_accessed=450_000, transcendentals=0),
        name="plane_sums",
    )(value)


def exchanged(value, axes):
    return lax.all_to_all(value, axes, 0, 0, tiled=True)


def after(value, *others):
    return lax.optimization_barrier((value, *others))[0]


def shards(inputs, out_grad, low_pass, high_pass, level_weight, mix):
    y, x, core = lax.axis_index("y"), lax.axis_index("x"), lax.axis_index("core")
    mine = x * NC + core
    place = jnp.stack([y, x, core]).astype(jnp.int32)

    one, three, two, grad_z = partials(place, mix, out_grad)
    arrived = [shift(value, "y", steps) for value, steps in ((one, 1), (three, 3), (two, 2))]

    own = exchanged(spread(after(inputs, grad_z)), PLANE)
    halo = shift(own, "z", 1, wrap=False)
    grad_z = exchanged(spread(grad_z, *arrived), PLANE)

    near = [shift(out_grad, "x", steps) for steps in (1, 3)]
    far = shift(after(out_grad, arrived[0]), "x", 2)
    early = [out_grad, shift(after(out_grad, own), "core", 1), far, shift(far, "core", 1)]
    grad_z, *early = lax.optimization_barrier((grad_z, *early))

    own_rows = [low_pass * R, level_weight[1:] * (R * high_pass[0]), level_weight[1:] * (R * high_pass[1])]
    own_rows += [level_weight[:1], R * high_pass, level_weight[1:]]
    table = jnp.concatenate(own_rows, 0)
    table = lax.dynamic_slice_in_dim(table.reshape(-1, 2, 8, 32), mine, 1, 2).reshape(-1, 64)
    coef = jnp.pad(table, ((0, 128 - table.shape[0]), (0, 0))).T

    z, slope, levels = forward(own, halo, coef)
    z_all = [z] + [shift(z, "y", steps) for steps in (1, 3, 2)]

    grad_mixed = (grad_z.astype(F32) * slope).astype(BF16)
    grad_halo = shift(grad_mixed, "z", -1, wrap=False)
    grad_in = backward(grad_mixed, grad_halo, own, levels, coef)
    og = early[:2]
    for piece in near:
        og += [piece, shift(after(piece, grad_in), "core", 1)]
    og += early[2:]
    grad_in = exchanged(grad_in, PLANE)
    part = product(place, z_all, og)
    grad_mix, low, high, level = plane_sums(exchanged(packed(part, grad_in), "z"))
    return gathered(grad_in), low, high, level, grad_mix


def solution(mesh):
    mesh = Mesh(mesh.devices.reshape(NZ, NX, NC, NY), ("z", "x", "core", "y"))
    wide, tall = P("y", CTX), P(None, "y")
    return jax.shard_map(
        shards,
        mesh=mesh,
        in_specs=(wide, wide, tall, tall, tall, tall),
        out_specs=(wide, tall, tall, tall, P(CTX, "y")),
        check_vma=False,
    )
```
